32 devices in a mesh: row: 2 (over core), col: 4 (over z), rep: 4 (over y, x).
Axes of the slice: x: 2, y: 2, z: 4, core: 2. Of those that a mesh axis runs over, the one named last changes fastest.
Arguments:
- amplitudes: bfloat16 [1024, 4, 1792], P('row', 'rep', 'col'), may hold values from -6 to 6
- integrals: bfloat16 [4, 1792, 8, 512], P('rep', 'row', 'col'), may hold values from -0.0625 to 0.0625
- cycle_weight: bfloat16 [1792, 512], replicated, may hold values from -0.125 to 0.125
- amplitude_mask: int32 [8, 4, 14], replicated, may hold values 0 or 1
- integral_mask: int32 [4, 14, 8, 4], replicated, may hold values 0 or 1
- cycle_order: int32 [8], replicated, may hold values from 0 to 7, as said below
Outputs:
- ladder_residual: bfloat16 [1024, 8, 512], P(('row', 'rep'), 'col')
- cycle_residual: bfloat16 [1024, 4, 512], P(('row', 'col'), 'rep')
The draws below stay inside these ranges and needn't reach their ends.
Inputs may be any that keep to these rules, and one draw needn't show every extreme that they name: cycle_order names every tile once; entries k * 4 to (k + 1) * 4 - 1 are a permutation of those same tile numbers.
All inputs are finite; a program needn't handle non-finite values.
Results may differ from the reference program's by a relative error of at most 0.0014.
Values may be sent and summed in bfloat16 or wider, within the bound.
A program may use at most 128 MiB of HBM per device.

```python
import jax
import jax.numpy as jnp
from jax import lax

TILE = 128
NVIRT = 1792
QB = 512
PR = 512
P_SIZE = 1024
PT = 8
CB = 4
QA = 8
DT = 14
QBT = 4


def draw_cycle_order(key, part):
    block_tiles = PR // TILE
    block_count = P_SIZE // PR
    block_keys = jax.random.split(key, block_count)
    orders = jax.vmap(lambda block_key: jax.random.permutation(block_key, block_tiles))(block_keys)
    offsets = (jnp.arange(block_count, dtype=jnp.int32) * block_tiles)[:, None]
    return (orders.astype(jnp.int32) + offsets).reshape(-1).astype(jnp.int32)


def touch_ends(array, own_key, least, largest):
    shape = array.shape
    spot = [jax.random.randint(jax.random.fold_in(own_key, axis), (), 0, shape[axis]) for axis in range(len(shape))]
    array = array.at[tuple(spot)].set(least)
    longest = shape.index(max(shape))
    spot[longest] = (spot[longest] + 1) % shape[longest]
    return array.at[tuple(spot)].set(largest)


def levels(key, shape, cuts, smallest, largest):
    factor_of = 1.0
    for axis_at, blocks in cuts:
        heights = jax.random.uniform(jax.random.fold_in(jax.random.fold_in(key, 6), axis_at), (blocks,), jnp.float32, smallest / len(cuts), largest / len(cuts))
        factor_of = factor_of * jnp.repeat(jnp.exp(heights), shape[axis_at] // blocks).reshape((-1,) + (1,) * (len(shape) - 1 - axis_at))
    return factor_of


def bell_draw(rng, shape, width, bound, shards=(), kind=jnp.bfloat16):
    result = jax.random.normal(rng, shape, jnp.float32) * width
    if len(shards) > 0:
        result = levels(rng, shape, shards, -0.22, 0.18) * result
    return jnp.clip(result, min=-bound, max=bound).astype(kind)


def setup_inputs(seed: int = 0) -> dict:
    seeds = jax.random.split(jax.random.key(seed), 7)
    amplitudes = bell_draw(seeds[0], (P_SIZE, CB, NVIRT), 1.0, 6.0, ((0, 2), (1, 4), (2, 4)))
    integrals = bell_draw(seeds[1], (CB, NVIRT, QA, QB), (CB * NVIRT) ** -0.5, 0.0625, ((0, 4), (1, 2), (2, 4)))
    cycle_weight = bell_draw(seeds[2], (NVIRT, QB), NVIRT ** -0.5, 0.125)
    amplitude_mask = touch_ends((jax.random.randint(seeds[3], (PT, CB, DT), 0, 3) < 2).astype(jnp.int32), jax.random.fold_in(seeds[3], 1), 0, 1)
    integral_mask = touch_ends((jax.random.randint(seeds[4], (CB, DT, QA, QBT), 0, 3) < 2).astype(jnp.int32), jax.random.fold_in(seeds[4], 1), 0, 1)
    cycle_order = draw_cycle_order(jax.random.fold_in(seeds[6], 71), 0)
    return {"amplitudes": amplitudes, "integrals": integrals, "cycle_weight": cycle_weight, "amplitude_mask": amplitude_mask, "integral_mask": integral_mask, "cycle_order": cycle_order}


def expand_tiles(tile_mask, axes_list):
    for axis_number in axes_list:
        tile_mask = jnp.repeat(tile_mask, TILE, axis=axis_number)
    return tile_mask


def reference(amplitudes, integrals, cycle_weight, amplitude_mask, integral_mask, cycle_order):
    zero_value = jnp.zeros((), jnp.bfloat16)
    masked_amps = jnp.where(expand_tiles(amplitude_mask, (0, 2)) > 0, amplitudes, zero_value)
    masked_ints = jnp.where(expand_tiles(integral_mask, (1, 3)) > 0, integrals, zero_value)
    flat_amps = masked_amps.reshape(P_SIZE, CB * NVIRT)
    slabs = jnp.transpose(masked_ints, (2, 0, 1, 3)).reshape(QA, CB * NVIRT, QB)

    def one_slab(panel_slab):
        return jnp.dot(flat_amps, panel_slab, preferred_element_type=jnp.float32).astype(jnp.bfloat16)

    ladder = jnp.transpose(lax.map(one_slab, slabs), (1, 0, 2))
    cycle_rows = masked_amps.reshape(PT, TILE, CB, NVIRT)[cycle_order].reshape(P_SIZE * CB, NVIRT)
    cycle = jnp.dot(cycle_rows, cycle_weight, preferred_element_type=jnp.float32).astype(jnp.bfloat16)
    return ladder, cycle.reshape(P_SIZE, CB, QB)
```

```python
import functools

import jax
import jax.numpy as jnp
from jax import lax
from jax.experimental import pallas as pl
from jax.experimental.pallas import tpu as pltpu
from jax.sharding import PartitionSpec as P

TILE = 128
HALF = TILE // 2
MESH = pl.DeviceIdType.MESH
VMEM_LIMIT = 40 * 2**20


def contract_with(panel, piece):
    return jnp.einsum("pcn,cnaq->paq", panel, piece, preferred_element_type=jnp.float32)


def apply_cycle(cycle_weight, gathered):
    return jnp.einsum(
        "pcd,de->pce", gathered, cycle_weight, preferred_element_type=jnp.float32
    ).astype(jnp.bfloat16)


def body(amplitudes, integrals, cycle_weight, amplitude_mask, integral_mask, cycle_order):
    row_count = amplitudes.shape[0]
    d_local = amplitudes.shape[2]
    d_rows = integrals.shape[1]
    a_local = integrals.shape[2]
    row_index = lax.axis_index("row")
    col_index = lax.axis_index("col")
    rep_index = lax.axis_index("rep")
    amp_tiles = row_count // TILE
    zero_value = jnp.zeros((), jnp.bfloat16)
    mask_rows = lax.dynamic_slice(
        amplitude_mask,
        (row_index * amp_tiles, rep_index, 0),
        (amp_tiles, 1, amplitude_mask.shape[2]),
    )
    amp_expanded = jnp.repeat(jnp.repeat(mask_rows, TILE, axis=0), TILE, axis=2)
    amp_local_mask = lax.dynamic_slice_in_dim(amp_expanded, col_index * d_local, d_local, 2)
    local_amps = jnp.where(amp_local_mask > 0, amplitudes, zero_value)
    slab_tiles = lax.dynamic_slice(
        integral_mask,
        (rep_index, 0, col_index * a_local, 0),
        (1, integral_mask.shape[1], a_local, integral_mask.shape[3]),
    )
    slab_expanded = jnp.repeat(jnp.repeat(slab_tiles, TILE, axis=1), TILE, axis=3)
    slab_local_mask = lax.dynamic_slice_in_dim(slab_expanded, row_index * d_rows, d_rows, 1)
    local_ints = jnp.where(slab_local_mask > 0, integrals, zero_value)
    local_order = (
        lax.dynamic_slice_in_dim(cycle_order, row_index * amp_tiles, amp_tiles)
        - row_index * amp_tiles
    )
    spread = lax.all_to_all(local_amps, "rep", split_axis=0, concat_axis=1, tiled=True)
    panel = lax.all_gather(spread, "col", axis=2, tiled=True)
    all_slabs = lax.all_gather(local_ints, "rep", axis=0, tiled=True)
    totals = contract_with(panel, lax.all_gather(all_slabs, "row", axis=1, tiled=True))
    ladder = totals.astype(jnp.bfloat16)
    permuted = local_amps.reshape(amp_tiles, TILE, 1, d_local)[local_order].reshape(
        row_count, 1, d_local
    )
    cycle = apply_cycle(
        cycle_weight, lax.all_to_all(permuted, "col", split_axis=0, concat_axis=2, tiled=True)
    )
    return (ladder, cycle)


def fused_kernel(
    cols,
    amps_ref,
    ints_ref,
    weight_ref,
    amp_mask,
    int_mask,
    order,
    ladder_ref,
    cycle_ref,
    panel,
    masked,
    slab,
    weight,
    partial,
    relayed,
    incoming,
    local_sem,
    pair_sem,
    send_sem,
    recv_sem,
    part_send,
    part_recv,
):
    d_local = amps_ref.shape[0]
    a_local, d_rows, width = ints_ref.shape
    d_tiles = masked.shape[1] // TILE
    b_tiles = width // TILE
    tiles = masked.shape[0]
    row, col, rep = (lax.axis_index(name) for name in ("row", "col", "rep"))
    order_of = (3, 1, 2, 0)

    barrier = pltpu.get_barrier_semaphore()
    pl.semaphore_signal(barrier, inc=1, device_id={"row": 1 - row}, device_id_type=MESH)
    for flip in order_of[:3]:
        pl.semaphore_signal(barrier, inc=1, device_id={"rep": rep ^ flip}, device_id_type=MESH)

    @pl.when(col > 0)
    def _():
        pl.semaphore_signal(barrier, inc=1, device_id={"col": col - 1}, device_id_type=MESH)

    @pl.when(col < cols - 1)
    def _():
        pl.semaphore_signal(barrier, inc=1, device_id={"col": col + 1}, device_id_type=MESH)

    def tile_of(k):
        return rep ^ order_of[k]

    def lanes(tile):
        return pl.ds(pl.multiple_of(tile * TILE, TILE), TILE)

    my_rows = pl.ds(pl.multiple_of(row * d_rows, TILE), d_rows)
    copy_ints = pltpu.make_async_copy(ints_ref, slab.at[:, my_rows, :], local_sem.at[0])
    copy_weight = pltpu.make_async_copy(weight_ref, weight, local_sem.at[1])
    copy_amps = [
        pltpu.make_async_copy(
            amps_ref.at[:, lanes(tile_of(k))], panel.at[tile_of(k), col], local_sem.at[2 + k]
        )
        for k in range(tiles)
    ]
    for copy in [copy_amps[0], copy_ints] + copy_amps[1:] + [copy_weight]:
        copy.start()

    pl.semaphore_wait(barrier, 4 + (col > 0).astype(jnp.int32) + (col < cols - 1).astype(jnp.int32))

    def hop(way, k, distance):
        step = 1 if way == 0 else -1
        source = col - step * distance
        slot = panel.at[tile_of(k), source]
        return pltpu.make_async_remote_copy(
            src_ref=amps_ref.at[:, lanes(tile_of(k))] if distance == 0 else slot,
            dst_ref=slot,
            send_sem=send_sem.at[way, k, distance],
            recv_sem=recv_sem.at[way, k, distance],
            device_id={"col": col + step},
            device_id_type=MESH,
        )

    def sends(way, distance):
        if way == 0:
            return (col >= distance) & (col < cols - 1)
        return (col + distance < cols) & (col > 0)

    def receives(way, distance):
        return (col > distance) if way == 0 else (col + distance < cols - 1)

    def start_hop(k, distance):
        for way in range(2):
            @pl.when(sends(way, distance))
            def _():
                hop(way, k, distance).start()

    def start_own(k, busy):
        for way in range(2):
            forwards = col if way == 0 else cols - 1 - col

            @pl.when(sends(way, 0) & ((forwards >= 2) if busy else (forwards < 2)))
            def _():
                hop(way, k, 0).start()

    def await_hop(k, distance):
        for way in range(2):
            step = 1 if way == 0 else -1

            @pl.when(receives(way, distance))
            def _():
                slot = panel.at[tile_of(k), col - step * (distance + 1)]
                pltpu.make_async_remote_copy(
                    src_ref=slot,
                    dst_ref=slot,
                    send_sem=send_sem.at[way, k, distance],
                    recv_sem=recv_sem.at[way, k, distance],
                    device_id={"col": col},
                    device_id_type=MESH,
                ).wait_recv()

    start_hop(0, 0)
    pair = pltpu.make_async_remote_copy(
        src_ref=ints_ref,
        dst_ref=slab.at[:, my_rows, :],
        send_sem=pair_sem.at[0],
        recv_sem=pair_sem.at[1],
        device_id={"row": 1 - row},
        device_id_type=MESH,
    )
    pair.start()

    def part_copy(k, a):
        if k == 0:
            target, landing = rep ^ (1 + a), relayed.at[a]
        else:
            target, landing = rep ^ k, incoming.at[k - 1, a]
        return pltpu.make_async_remote_copy(
            src_ref=partial.at[k, a],
            dst_ref=landing,
            send_sem=part_send.at[k, a],
            recv_sem=part_recv.at[k, a],
            device_id={"rep": target},
            device_id_type=MESH,
        )

    def pass_on(k, a):
        part_copy(0, a).wait_recv()
        partial[k, a] += relayed[a]
        part_copy(k, a).start()

    zero = jnp.zeros((TILE, TILE), jnp.bfloat16)

    def mask_ints(tile, carry):
        rows = pl.ds(pl.multiple_of(tile * TILE, TILE), TILE)
        for a in range(a_local):
            for b in range(b_tiles):
                keep = int_mask[rep, col * a_local + a, b, tile] > 0
                spot = pl.ds(b * TILE, TILE)
                slab[a, rows, spot] = jnp.where(keep, slab[a, rows, spot], zero)
        return carry

    strip = jnp.zeros((HALF, TILE), jnp.bfloat16)

    def block_product(k, source, first):
        tile = tile_of(k)
        for j in range(d_local // HALF):
            keep = amp_mask[row * tiles + tile, rep, (source * d_local + j * HALF) // TILE] > 0
            spot = pl.ds(pl.multiple_of(source * d_local + j * HALF, HALF), HALF)
            masked[tile, spot, :] = jnp.where(
                keep, panel[tile, source, pl.ds(j * HALF, HALF), :], strip
            )
        depth = pl.ds(pl.multiple_of(source * d_local, HALF), d_local)
        for a in range(a_local):
            product = lax.dot_general(
                masked[tile, depth, :],
                slab[a, depth, :],
                (((0,), (0,)), ((), ())),
                preferred_element_type=jnp.float32,
            )
            if first:
                partial[k, a] = product
            else:
                partial[k, a] += product

    for k in range(tiles):
        if k + 1 < tiles:
            start_own(k + 1, False)
        copy_amps[k].wait()
        if k > 0:
            block_product(k, col, True)
        for distance in range(cols - 1):
            await_hop(k, distance)
            if distance < cols - 2:
                start_hop(k, distance + 1)
            if distance == 0:
                if k + 1 < tiles:
                    start_own(k + 1, True)
                if k == 0:
                    copy_ints.wait()
                    pair.wait()
                    lax.fori_loop(0, d_tiles, mask_ints, 0)
                    block_product(k, col, True)
                if k == 2:
                    pass_on(1, 1)
            for way in range(2):
                @pl.when(receives(way, distance))
                def _():
                    block_product(k, col - (1 if way == 0 else -1) * (distance + 1), False)
        if k == 0:
            part_copy(0, 0).start()
            part_copy(0, 1).start()
        elif k == 1:
            part_copy(1, 0).start()
        elif k == 2:
            part_copy(2, 1).start()
            pass_on(2, 0)

    copy_weight.wait()
    place = lax.rem(order[row * tiles + col], tiles)
    cycle_ref[...] = lax.dot_general(
        masked[place], weight[...], (((0,), (0,)), ((), ())), preferred_element_type=jnp.float32
    ).astype(jnp.bfloat16)
    for a in (0, 1):
        part_copy(1, a).wait_recv()
        partial[3, a] += incoming[0, a]
    for a in (1, 0):
        part_copy(2, a).wait_recv()
        ladder_ref[a] = (partial[3, a] + incoming[1, a]).astype(jnp.bfloat16)
    for k in range(tiles - 1):
        for a in range(a_local):
            part_copy(k, a).wait_send()
    for k in range(tiles):
        for distance in range(cols - 1):
            for way in range(2):
                @pl.when(sends(way, distance))
                def _():
                    hop(way, k, distance).wait_send()


def fused_body(cols, amplitudes, integrals, cycle_weight, amplitude_mask, integral_mask, cycle_order):
    rows, _, d_local = amplitudes.shape
    _, d_rows, a_local, width = integrals.shape
    depth = cols * d_local
    tiles = rows // TILE
    amps = jnp.transpose(amplitudes, (1, 2, 0)).reshape(d_local, rows)
    ints = jnp.transpose(integrals, (0, 2, 1, 3)).reshape(a_local, d_rows, width)
    anywhere = pl.BlockSpec(memory_space=pl.ANY)
    scalars = pl.BlockSpec(memory_space=pltpu.SMEM)
    in_vmem = pl.BlockSpec(memory_space=pltpu.VMEM)
    ladder, cycle = pl.pallas_call(
        functools.partial(fused_kernel, cols),
        out_shape=(
            jax.ShapeDtypeStruct((a_local, TILE, width), jnp.bfloat16),
            jax.ShapeDtypeStruct((TILE, width), jnp.bfloat16),
        ),
        in_specs=[anywhere] * 3 + [scalars] * 3,
        out_specs=(in_vmem, in_vmem),
        scratch_shapes=[
            pltpu.VMEM((tiles, cols, d_local, TILE), jnp.bfloat16),
            pltpu.VMEM((tiles, depth, TILE), jnp.bfloat16),
            pltpu.VMEM((a_local, depth, width), jnp.bfloat16),
            pltpu.VMEM((depth, width), jnp.bfloat16),
            pltpu.VMEM((tiles, a_local, TILE, width), jnp.float32),
            pltpu.VMEM((a_local, TILE, width), jnp.float32),
            pltpu.VMEM((2, a_local, TILE, width), jnp.float32),
            pltpu.SemaphoreType.DMA((2 + tiles,)),
            pltpu.SemaphoreType.DMA((2,)),
            pltpu.SemaphoreType.DMA((2, tiles, cols - 1)),
            pltpu.SemaphoreType.DMA((2, tiles, cols - 1)),
            pltpu.SemaphoreType.DMA((tiles - 1, a_local)),
            pltpu.SemaphoreType.DMA((tiles - 1, a_local)),
        ],
        compiler_params=pltpu.CompilerParams(
            collective_id=0, has_side_effects=True, vmem_limit_bytes=VMEM_LIMIT
        ),
        name="ladder_and_cycle",
    )(amps, ints, cycle_weight, amplitude_mask, jnp.transpose(integral_mask, (0, 2, 3, 1)), cycle_order)
    return jnp.transpose(ladder, (1, 0, 2)), cycle[:, None, :]


def fits_fused(mesh, amplitudes, integrals):
    rows = amplitudes.shape[0] // mesh.shape["row"]
    d_local = amplitudes.shape[2] // mesh.shape["col"]
    return (
        mesh.shape["row"] == 2
        and mesh.shape["rep"] == 4
        and rows == mesh.shape["rep"] * TILE
        and rows == mesh.shape["col"] * TILE
        and d_local % HALF == 0
        and integrals.shape[2] == 2 * mesh.shape["col"]
        and integrals.shape[1] // mesh.shape["row"] % TILE == 0
    )


def solution(mesh):
    placed = (P("row", "rep", "col"), P("rep", "row", "col", None), P(), P(), P(), P())

    def run(*arrays):
        fused = fits_fused(mesh, *arrays[:2])
        return jax.shard_map(
            functools.partial(fused_body, mesh.shape["col"]) if fused else body,
            mesh=mesh,
            in_specs=placed,
            out_specs=(P(("row", "rep"), "col", None), P(("row", "col"), "rep", None)),
            check_vma=False,
        )(*arrays)

    return run
```

```python
import functools

import jax
import jax.numpy as jnp
from jax import lax
from jax.experimental import pallas as pl
from jax.experimental.pallas import tpu as pltpu
from jax.sharding import PartitionSpec as P

TILE = 128
HALF = TILE // 2
MESH = pl.DeviceIdType.MESH
VMEM_LIMIT = 40 * 2**20


def contract_with(panel, piece):
    return jnp.einsum("pcn,cnaq->paq", panel, piece, preferred_element_type=jnp.float32)


def apply_cycle(cycle_weight, gathered):
    return jnp.einsum(
        "pcd,de->pce", gathered, cycle_weight, preferred_element_type=jnp.float32
    ).astype(jnp.bfloat16)


def body(amplitudes, integrals, cycle_weight, amplitude_mask, integral_mask, cycle_order):
    row_count = amplitudes.shape[0]
    d_local = amplitudes.shape[2]
    d_rows = integrals.shape[1]
    a_local = integrals.shape[2]
    row_index = lax.axis_index("row")
    col_index = lax.axis_index("col")
    rep_index = lax.axis_index("rep")
    amp_tiles = row_count // TILE
    zero_value = jnp.zeros((), jnp.bfloat16)
    mask_rows = lax.dynamic_slice(
        amplitude_mask,
        (row_index * amp_tiles, rep_index, 0),
        (amp_tiles, 1, amplitude_mask.shape[2]),
    )
    amp_expanded = jnp.repeat(jnp.repeat(mask_rows, TILE, axis=0), TILE, axis=2)
    amp_local_mask = lax.dynamic_slice_in_dim(amp_expanded, col_index * d_local, d_local, 2)
    local_amps = jnp.where(amp_local_mask > 0, amplitudes, zero_value)
    slab_tiles = lax.dynamic_slice(
        integral_mask,
        (rep_index, 0, col_index * a_local, 0),
        (1, integral_mask.shape[1], a_local, integral_mask.shape[3]),
    )
    slab_expanded = jnp.repeat(jnp.repeat(slab_tiles, TILE, axis=1), TILE, axis=3)
    slab_local_mask = lax.dynamic_slice_in_dim(slab_expanded, row_index * d_rows, d_rows, 1)
    local_ints = jnp.where(slab_local_mask > 0, integrals, zero_value)
    local_order = (
        lax.dynamic_slice_in_dim(cycle_order, row_index * amp_tiles, amp_tiles)
        - row_index * amp_tiles
    )
    spread = lax.all_to_all(local_amps, "rep", split_axis=0, concat_axis=1, tiled=True)
    panel = lax.all_gather(spread, "col", axis=2, tiled=True)
    all_slabs = lax.all_gather(local_ints, "rep", axis=0, tiled=True)
    totals = contract_with(panel, lax.all_gather(all_slabs, "row", axis=1, tiled=True))
    ladder = totals.astype(jnp.bfloat16)
    permuted = local_amps.reshape(amp_tiles, TILE, 1, d_local)[local_order].reshape(
        row_count, 1, d_local
    )
    cycle = apply_cycle(
        cycle_weight, lax.all_to_all(permuted, "col", split_axis=0, concat_axis=2, tiled=True)
    )
    return (ladder, cycle)


def fused_kernel(
    cols,
    amps_ref,
    ints_ref,
    weight_ref,
    amp_mask,
    int_mask,
    order,
    ladder_ref,
    cycle_ref,
    panel,
    masked,
    slab,
    weight,
    partial,
    relayed,
    incoming,
    chosen,
    cycle_sum,
    local_sem,
    pair_sem,
    send_sem,
    recv_sem,
    part_send,
    part_recv,
):
    d_local = amps_ref.shape[0]
    a_local, d_rows, width = ints_ref.shape
    d_tiles = masked.shape[1] // TILE
    b_tiles = width // TILE
    tiles = masked.shape[0]
    row, col, rep = (lax.axis_index(name) for name in ("row", "col", "rep"))
    order_of = (3, 1, 2, 0)

    barrier = pltpu.get_barrier_semaphore()
    pl.semaphore_signal(barrier, inc=1, device_id={"row": 1 - row}, device_id_type=MESH)
    for flip in order_of[:3]:
        pl.semaphore_signal(barrier, inc=1, device_id={"rep": rep ^ flip}, device_id_type=MESH)

    @pl.when(col > 0)
    def _():
        pl.semaphore_signal(barrier, inc=1, device_id={"col": col - 1}, device_id_type=MESH)

    @pl.when(col < cols - 1)
    def _():
        pl.semaphore_signal(barrier, inc=1, device_id={"col": col + 1}, device_id_type=MESH)

    def tile_of(k):
        return rep ^ order_of[k]

    def lanes(tile):
        return pl.ds(pl.multiple_of(tile * TILE, TILE), TILE)

    my_rows = pl.ds(pl.multiple_of(row * d_rows, TILE), d_rows)
    copy_ints = pltpu.make_async_copy(ints_ref, slab.at[:, my_rows, :], local_sem.at[0])
    copy_weight = pltpu.make_async_copy(weight_ref, weight, local_sem.at[1])
    copy_amps = [
        pltpu.make_async_copy(
            amps_ref.at[:, lanes(tile_of(k))], panel.at[tile_of(k), col], local_sem.at[2 + k]
        )
        for k in range(tiles)
    ]
    for copy in [copy_amps[0], copy_ints] + copy_amps[1:] + [copy_weight]:
        copy.start()

    pl.semaphore_wait(barrier, 4 + (col > 0).astype(jnp.int32) + (col < cols - 1).astype(jnp.int32))

    def hop(way, k, distance):
        step = 1 if way == 0 else -1
        source = col - step * distance
        slot = panel.at[tile_of(k), source]
        return pltpu.make_async_remote_copy(
            src_ref=slot,
            dst_ref=slot,
            send_sem=send_sem.at[way, k, distance],
            recv_sem=recv_sem.at[way, k, distance],
            device_id={"col": col + step},
            device_id_type=MESH,
        )

    def sends(way, distance):
        if way == 0:
            return (col >= distance) & (col < cols - 1)
        return (col + distance < cols) & (col > 0)

    def receives(way, distance):
        return (col > distance) if way == 0 else (col + distance < cols - 1)

    def start_hop(k, distance):
        for way in range(2):
            @pl.when(sends(way, distance))
            def _():
                hop(way, k, distance).start()

    def start_own(k, busy):
        for way in range(2):
            forwards = col if way == 0 else cols - 1 - col

            @pl.when(sends(way, 0) & ((forwards >= 2) if busy else (forwards < 2)))
            def _():
                hop(way, k, 0).start()

    def await_hop(k, distance):
        for way in range(2):
            step = 1 if way == 0 else -1

            @pl.when(receives(way, distance))
            def _():
                slot = panel.at[tile_of(k), col - step * (distance + 1)]
                pltpu.make_async_remote_copy(
                    src_ref=slot,
                    dst_ref=slot,
                    send_sem=send_sem.at[way, k, distance],
                    recv_sem=recv_sem.at[way, k, distance],
                    device_id={"col": col},
                    device_id_type=MESH,
                ).wait_recv()

    copy_amps[0].wait()
    start_hop(0, 0)
    copy_amps[1].wait()
    start_own(1, True)
    pair = pltpu.make_async_remote_copy(
        src_ref=ints_ref,
        dst_ref=slab.at[:, my_rows, :],
        send_sem=pair_sem.at[0],
        recv_sem=pair_sem.at[1],
        device_id={"row": 1 - row},
        device_id_type=MESH,
    )
    pair.start()

    def part_copy(k, a):
        if k == 0:
            target, landing = rep ^ (1 + a), relayed.at[a]
        else:
            target, landing = rep ^ k, incoming.at[k - 1, a]
        return pltpu.make_async_remote_copy(
            src_ref=partial.at[k, a],
            dst_ref=landing,
            send_sem=part_send.at[k, a],
            recv_sem=part_recv.at[k, a],
            device_id={"rep": target},
            device_id_type=MESH,
        )

    def pass_on(k, a):
        part_copy(0, a).wait_recv()
        partial[k, a] += relayed[a]
        part_copy(k, a).start()

    zero = jnp.zeros((TILE, TILE), jnp.bfloat16)

    def mask_ints(tile, carry):
        rows = pl.ds(pl.multiple_of(tile * TILE, TILE), TILE)
        for a in range(a_local):
            for b in range(b_tiles):
                keep = int_mask[rep, col * a_local + a, b, tile] > 0
                spot = pl.ds(b * TILE, TILE)
                slab[a, rows, spot] = jnp.where(keep, slab[a, rows, spot], zero)
        return carry

    strip = jnp.zeros((HALF, TILE), jnp.bfloat16)
    place = lax.rem(order[row * tiles + col], tiles)
    copy_weight.wait()

    def block_product(k, source, first):
        tile = tile_of(k)
        for j in range(d_local // HALF):
            keep = amp_mask[row * tiles + tile, rep, (source * d_local + j * HALF) // TILE] > 0
            spot = pl.ds(pl.multiple_of(source * d_local + j * HALF, HALF), HALF)
            piece = jnp.where(keep, panel[tile, source, pl.ds(j * HALF, HALF), :], strip)
            masked[tile, spot, :] = piece
            chosen[spot, :] = jnp.where(place == tile, piece, strip if k == 0 else chosen[spot, :])
        depth = pl.ds(pl.multiple_of(source * d_local, HALF), d_local)
        for a in range(a_local):
            product = lax.dot_general(
                masked[tile, depth, :],
                slab[a, depth, :],
                (((0,), (0,)), ((), ())),
                preferred_element_type=jnp.float32,
            )
            if first:
                partial[k, a] = product
            else:
                partial[k, a] += product
        if k == tiles - 1:
            product = lax.dot_general(
                chosen[depth, :],
                weight[depth, :],
                (((0,), (0,)), ((), ())),
                preferred_element_type=jnp.float32,
            )
            if first:
                cycle_sum[...] = product
            else:
                cycle_sum[...] += product

    for k in range(tiles):
        if k + 1 < tiles:
            if k > 0:
                copy_amps[k + 1].wait()
            start_own(k + 1, False)
        if k > 0:
            block_product(k, col, True)
        for distance in range(cols - 1):
            if k == tiles - 1 and distance == cols - 2:
                for sender in (1, 2):
                    for a in range(a_local):
                        part_copy(sender, a).wait_recv()
                        partial[3, a] += incoming[sender - 1, a]
            await_hop(k, distance)
            if distance < cols - 2:
                start_hop(k, distance + 1)
            if distance == 0:
                if 0 < k < tiles - 1:
                    start_own(k + 1, True)
                if k == 0:
                    copy_ints.wait()
                    pair.wait()
                    lax.fori_loop(0, d_tiles, mask_ints, 0)
                    block_product(k, col, True)
                if k == 2:
                    pass_on(1, 1)
            for way in range(2):
                @pl.when(receives(way, distance))
                def _():
                    block_product(k, col - (1 if way == 0 else -1) * (distance + 1), False)
        if k == 0:
            part_copy(0, 0).start()
            part_copy(0, 1).start()
        elif k == 1:
            part_copy(1, 0).start()
        elif k == 2:
            part_copy(2, 1).start()
            pass_on(2, 0)

    cycle_ref[...] = cycle_sum[...].astype(jnp.bfloat16)
    for a in range(a_local):
        ladder_ref[a] = partial[3, a].astype(jnp.bfloat16)
    for k in range(tiles - 1):
        for a in range(a_local):
            part_copy(k, a).wait_send()
    for k in range(tiles):
        for distance in range(cols - 1):
            for way in range(2):
                @pl.when(sends(way, distance))
                def _():
                    hop(way, k, distance).wait_send()


def fused_body(cols, amplitudes, integrals, cycle_weight, amplitude_mask, integral_mask, cycle_order):
    rows, _, d_local = amplitudes.shape
    _, d_rows, a_local, width = integrals.shape
    depth = cols * d_local
    tiles = rows // TILE
    amps = jnp.transpose(amplitudes, (1, 2, 0)).reshape(d_local, rows)
    ints = jnp.transpose(integrals, (0, 2, 1, 3)).reshape(a_local, d_rows, width)
    anywhere = pl.BlockSpec(memory_space=pl.ANY)
    scalars = pl.BlockSpec(memory_space=pltpu.SMEM)
    in_vmem = pl.BlockSpec(memory_space=pltpu.VMEM)
    ladder, cycle = pl.pallas_call(
        functools.partial(fused_kernel, cols),
        out_shape=(
            jax.ShapeDtypeStruct((a_local, TILE, width), jnp.bfloat16),
            jax.ShapeDtypeStruct((TILE, width), jnp.bfloat16),
        ),
        in_specs=[anywhere] * 3 + [scalars] * 3,
        out_specs=(in_vmem, in_vmem),
        scratch_shapes=[
            pltpu.VMEM((tiles, cols, d_local, TILE), jnp.bfloat16),
            pltpu.VMEM((tiles, depth, TILE), jnp.bfloat16),
            pltpu.VMEM((a_local, depth, width), jnp.bfloat16),
            pltpu.VMEM((depth, width), jnp.bfloat16),
            pltpu.VMEM((tiles, a_local, TILE, width), jnp.float32),
            pltpu.VMEM((a_local, TILE, width), jnp.float32),
            pltpu.VMEM((2, a_local, TILE, width), jnp.float32),
            pltpu.VMEM((depth, TILE), jnp.bfloat16),
            pltpu.VMEM((TILE, width), jnp.float32),
            pltpu.SemaphoreType.DMA((2 + tiles,)),
            pltpu.SemaphoreType.DMA((2,)),
            pltpu.SemaphoreType.DMA((2, tiles, cols - 1)),
            pltpu.SemaphoreType.DMA((2, tiles, cols - 1)),
            pltpu.SemaphoreType.DMA((tiles - 1, a_local)),
            pltpu.SemaphoreType.DMA((tiles - 1, a_local)),
        ],
        compiler_params=pltpu.CompilerParams(
            collective_id=0, has_side_effects=True, vmem_limit_bytes=VMEM_LIMIT
        ),
        name="ladder_and_cycle",
    )(amps, ints, cycle_weight, amplitude_mask, jnp.transpose(integral_mask, (0, 2, 3, 1)), cycle_order)
    return jnp.transpose(ladder, (1, 0, 2)), cycle[:, None, :]


def fits_fused(mesh, amplitudes, integrals):
    rows = amplitudes.shape[0] // mesh.shape["row"]
    d_local = amplitudes.shape[2] // mesh.shape["col"]
    return (
        mesh.shape["row"] == 2
        and mesh.shape["rep"] == 4
        and rows == mesh.shape["rep"] * TILE
        and rows == mesh.shape["col"] * TILE
        and d_local % HALF == 0
        and integrals.shape[2] == 2 * mesh.shape["col"]
        and integrals.shape[1] // mesh.shape["row"] % TILE == 0
    )


def solution(mesh):
    placed = (P("row", "rep", "col"), P("rep", "row", "col", None), P(), P(), P(), P())

    def run(*arrays):
        fused = fits_fused(mesh, *arrays[:2])
        return jax.shard_map(
            functools.partial(fused_body, mesh.shape["col"]) if fused else body,
            mesh=mesh,
            in_specs=placed,
            out_specs=(P(("row", "rep"), "col", None), P(("row", "col"), "rep", None)),
            check_vma=False,
        )(*arrays)

    return run
```
